32 devices in a mesh: seq: 32 (over z, y, x, core).
Axes of the slice: x: 2, y: 2, z: 4, core: 2. Of those that a mesh axis runs over, the one named last changes fastest.
Arguments:
- queries: bfloat16 [6144, 1024], P('seq'), may hold values from -200 to 200
- keyval: bfloat16 [2, 6144, 128], P(None, 'seq'), may hold values from -7 to 7
Outputs:
- attended: bfloat16 [6144, 1024], P('seq')
The draws below stay inside these ranges and needn't reach their ends.
All inputs are finite; a program needn't handle non-finite values.
Results may differ from the reference program's by a relative error of at most 0.0029.
Values may be sent and summed in bfloat16 or wider, within the bound.
No kernel may reach another device: no remote copies, remote signals or barrier semaphores. Data moves between devices by JAX's collectives and lax.ppermute only.
A program may use at most 64 MiB of HBM per device.

```python
import jax
import jax.numpy as jnp
from jax import lax

QH = 8
KVH = 1
HD = 128
TOK_DEV = 192
LEVELS = 5
TOKENS = 6144
N_SEQ = 32


def shared_keys(key):
    base = jax.random.truncated_normal(jax.random.fold_in(key, 7), -6.0, 6.0, (2, TOKENS, KVH * HD), jnp.float32)
    return base


def draw_keyval(key, part):
    return shared_keys(key).astype(jnp.bfloat16)


def draw_queries(key, part):
    values = 3.0 * jax.random.truncated_normal(jax.random.fold_in(key, 9), -6.0, 6.0, (TOKENS, QH * HD), jnp.float32)
    return values.astype(jnp.bfloat16)


def setup_inputs(seed: int = 0) -> dict:
    arg_keys = jax.random.split(jax.random.key(seed), 3)
    return {
        "queries": draw_queries(jax.random.fold_in(arg_keys[2], 71), 0),
        "keyval": draw_keyval(jax.random.fold_in(arg_keys[2], 71), 0),
    }


def attend(queries, keyval):
    tok = queries.shape[0]
    total = keyval.shape[1]
    group = QH // KVH
    scale = 1.0 / (HD ** 0.5)
    qs = jnp.moveaxis(queries.reshape(tok, KVH, group * HD), 1, 0)
    ks = jnp.moveaxis(keyval[0].reshape(total, KVH, HD), 1, 0)
    vs = jnp.moveaxis(keyval[1].reshape(total, KVH, HD), 1, 0)

    def per_head(items):
        q_group, k_head, v_head = items
        q_group = q_group.reshape(tok, group, HD).astype(jnp.float32)
        scores = jnp.einsum("tqd,sd->qts", q_group, k_head.astype(jnp.float32)) * scale
        top = jnp.max(scores, axis=2, keepdims=True)
        probs = jnp.exp(scores - top)
        totals = jnp.sum(probs, axis=2)
        weights = probs.astype(jnp.bfloat16).astype(jnp.float32)
        summed = jnp.einsum("qts,sd->tqd", weights, v_head.astype(jnp.float32))
        return summed / jnp.moveaxis(totals, 0, 1)[:, :, None]

    outs = lax.map(per_head, (qs, ks, vs))
    return jnp.moveaxis(outs, 0, 1).reshape(tok, QH * HD).astype(jnp.bfloat16)


def reference(queries, keyval):
    blocks = N_SEQ
    width = keyval.shape[2]
    kv_blocks = keyval.reshape(2, blocks, TOK_DEV, width)
    q_blocks = queries.reshape(blocks, TOK_DEV, QH * HD)
    powers = jnp.array([2 ** j for j in range(LEVELS)], dtype=jnp.int32)

    def one_block(index):
        partners = jnp.bitwise_xor(index, powers)
        chosen = jnp.concatenate([index.reshape(1), partners, jnp.zeros((1,), jnp.int32)]).astype(jnp.int32)
        keys = kv_blocks[:, chosen].reshape(2, (LEVELS + 2) * TOK_DEV, width)
        q_block = lax.dynamic_index_in_dim(q_blocks, index, 0, keepdims=False)
        return attend(q_block, keys)

    result = lax.map(one_block, jnp.arange(blocks, dtype=jnp.int32))
    return result.reshape(blocks * TOK_DEV, QH * HD)
```

```python
import functools
import math

import jax
import jax.numpy as jnp
from jax import lax
from jax.experimental import pallas as pl
from jax.experimental.pallas import tpu as pltpu
from jax.sharding import PartitionSpec as P

HD = 128
AXIS = "seq"
FANOUT = 2
PAIR = 2
LOG2E = math.log2(math.e)
VMEM = pl.BlockSpec(memory_space=pltpu.VMEM)


def hops(a, b):
    return (a ^ b).bit_count()


def fill(real, count):
    goes = dict(real)
    open_to = set(range(count)) - set(goes.values())
    late = []
    for i in range(count):
        if i in goes:
            continue
        if i ^ 1 in open_to:
            goes[i] = i ^ 1
            open_to.remove(i ^ 1)
        else:
            late.append(i)
    for i in late:
        goes[i] = min(sorted(open_to), key=lambda t: (t == i, hops(t, i), t))
        open_to.remove(goes[i])
    for i in range(count):
        if goes[i] == i:
            goes[i], goes[i ^ 1] = goes[i ^ 1], goes[i]
    return sorted(goes.items())


def plan(informed, count):
    informed = set(informed)
    missing = [t for t in range(0, count, 2) if t not in informed]
    waves = []
    while missing:
        sends = {s: [] for s in sorted(informed) if s}
        order = sorted(missing, key=lambda t: (-min(hops(s, t) for s in sends), -t))
        for t in order:
            free = [s for s in sends if len(sends[s]) < FANOUT]
            if not free:
                break
            s = min(free, key=lambda s: (hops(s, t), len(sends[s]), -s))
            sends[s].append(t)
        wave = [[(s, ts[k]) for s, ts in sends.items() if len(ts) > k] for k in range(FANOUT)]
        wave = [w for w in wave if w]
        waves.append(wave)
        reached = {t for w in wave for _, t in w}
        informed |= reached
        missing = [t for t in missing if t not in reached]
    return waves


def member(me, devices):
    hit = me == devices[0]
    for d in devices[1:]:
        hit = hit | (me == d)
    return hit


def attend_body(blocks, first, last, *refs):
    it = iter(refs)
    q_ref = next(it)
    kv = [next(it) for _ in range(blocks)]
    if not first:
        m_in, l_in, a_in = next(it), next(it), next(it)
    if last:
        o_ref = next(it)
    else:
        m_out, l_out, a_out = next(it), next(it), next(it)
    tok, width = q_ref.shape
    heads = width // HD
    group = math.gcd(heads, PAIR)
    keys = [r[0] for r in kv]
    vals = [r[1].T for r in kv]
    keys = keys[0] if blocks == 1 else jnp.concatenate(keys, axis=0)
    vals = vals[0] if blocks == 1 else jnp.concatenate(vals, axis=1)
    for g in range(0, heads, group):
        q = jnp.concatenate([q_ref[:, pl.ds(h * HD, HD)] for h in range(g, g + group)], axis=0)
        cols = pl.ds(g * tok, group * tok)
        s = lax.dot_general(keys, q, (((1,), (1,)), ((), ())), preferred_element_type=jnp.float32)
        s = s * (LOG2E / math.sqrt(HD))
        top = jnp.max(s, axis=0, keepdims=True)
        if not first:
            old = m_in[:, cols]
            top = jnp.maximum(old, top)
            alpha = jnp.exp2(old - top)
        p = jnp.exp2(s - top)
        total = jnp.sum(p, axis=0, keepdims=True)
        out = jnp.dot(vals, p.astype(jnp.bfloat16), preferred_element_type=jnp.float32)
        if not first:
            total = total + alpha * l_in[:, cols]
            out = out + alpha * a_in[:, cols]
        if last:
            out = (out / total).T.astype(o_ref.dtype)
            for h in range(group):
                o_ref[:, pl.ds((g + h) * HD, HD)] = out[h * tok : (h + 1) * tok]
        else:
            m_out[:, cols] = top
            l_out[:, cols] = total
            a_out[:, cols] = out


def attend(queries, blocks, state=None, last=False):
    tok, width = queries.shape
    rows = width // HD * tok
    if last:
        out_shape, out_specs = jax.ShapeDtypeStruct((tok, width), queries.dtype), VMEM
    else:
        out_shape = tuple(pltpu.VMEM((n, rows), jnp.float32) for n in (1, 1, HD))
        out_specs = (VMEM,) * 3
    args = [queries, *blocks, *(state or ())]
    args = [pltpu.with_memory_space_constraint(a, pltpu.VMEM) for a in args]
    pairs = rows * sum(b.shape[1] for b in blocks)
    return pl.pallas_call(
        functools.partial(attend_body, len(blocks), state is None, last),
        out_shape=out_shape,
        in_specs=[VMEM] * len(args),
        out_specs=out_specs,
        compiler_params=pltpu.CompilerParams(vmem_limit_bytes=24 << 20),
        cost_estimate=pl.CostEstimate(flops=4 * pairs * HD, bytes_accessed=0, transcendentals=pairs),
    )(*args)


def on_device(queries, keyval):
    count = lax.axis_size(AXIS)
    levels = count.bit_length() - 1
    me = lax.axis_index(AXIS)
    far = 3 << levels - 2

    def swap(value, bit):
        return lax.ppermute(value, AXIS, [(i, i ^ 1 << bit) for i in range(count)])

    def send(value, real):
        return lax.ppermute(value, AXIS, fill(real, count))

    received = {}
    first = None
    informed = [0, 1]
    for bit in [*range(levels - 1, max(levels - 3, 0), -1), None, *range(max(levels - 3, 0), 0, -1)]:
        if bit is None:
            got, holder = send(keyval, [(0, far)]), far
        else:
            got, holder = swap(keyval, bit), 1 << bit
            received[bit] = got
        informed.append(holder)
        first = got if first is None else jnp.where(me == holder, got, first)
    state = attend(queries, [keyval])
    for wave in plan(informed, count):
        came = [(send(first, real), [t for _, t in real]) for real in wave]
        for got, holders in came:
            first = jnp.where(member(me, holders), got, first)
    state = attend(queries, [received[bit] for bit in range(1, levels)], state)
    first = jnp.where(me == 0, keyval, first)
    both = swap(jnp.concatenate([keyval, first], axis=0), 0)
    first = jnp.where(me % 2 == 1, both[2:], first)
    return attend(queries, [both[:2], first], state, last=True)


def solution(mesh):
    return jax.shard_map(
        on_device,
        mesh=mesh,
        in_specs=(P(AXIS, None), P(None, AXIS, None)),
        out_specs=P(AXIS, None),
        check_vma=False,
    )
```

```python
import functools
import math

import jax
import jax.numpy as jnp
from jax import lax
from jax.experimental import pallas as pl
from jax.experimental.pallas import tpu as pltpu
from jax.sharding import PartitionSpec as P

HD = 128
AXIS = "seq"
FANOUT = 2
CHUNK = 512
LOG2E = math.log2(math.e)
VMEM = pl.BlockSpec(memory_space=pltpu.VMEM)


def hops(a, b):
    return (a ^ b).bit_count()


def fill(real, count):
    goes = dict(real)
    open_to = set(range(count)) - set(goes.values())
    late = []
    for i in range(count):
        if i in goes:
            continue
        if i ^ 1 in open_to:
            goes[i] = i ^ 1
            open_to.remove(i ^ 1)
        else:
            late.append(i)
    for i in late:
        goes[i] = min(sorted(open_to), key=lambda t: (t == i, hops(t, i), t))
        open_to.remove(goes[i])
    for i in range(count):
        if goes[i] == i:
            goes[i], goes[i ^ 1] = goes[i ^ 1], goes[i]
    return sorted(goes.items())


def plan(informed, count):
    informed = set(informed)
    missing = [t for t in range(0, count, 2) if t not in informed]
    waves = []
    while missing:
        sends = {s: [] for s in sorted(informed) if s}
        order = sorted(missing, key=lambda t: (-min(hops(s, t) for s in sends), -t))
        for t in order:
            free = [s for s in sends if len(sends[s]) < FANOUT]
            if not free:
                break
            s = min(free, key=lambda s: (hops(s, t), len(sends[s]), -s))
            sends[s].append(t)
        wave = [[(s, ts[k]) for s, ts in sends.items() if len(ts) > k] for k in range(FANOUT)]
        wave = [w for w in wave if w]
        waves.append(wave)
        reached = {t for w in wave for _, t in w}
        informed |= reached
        missing = [t for t in missing if t not in reached]
    return waves


def member(me, devices):
    hit = me == devices[0]
    for d in devices[1:]:
        hit = hit | (me == d)
    return hit


def chunk_of(rows):
    return max(c for c in range(HD, rows + 1, HD) if rows % c == 0 and (c <= CHUNK or c == HD))


def attend_body(blocks, first, last, carried, *refs):
    it = iter(refs)
    q_ref = next(it)
    kv = [next(it) for _ in range(blocks)]
    tok = kv[0].shape[1]
    if not first:
        m_in, l_in, a_in = next(it), next(it), next(it)
    if carried:
        carry_in = next(it)
    if last:
        o_ref = next(it)
    else:
        m_out, l_out, a_out = next(it), next(it), next(it)
    if carried:
        carry_out = next(it)
        carry_out[...] = carry_in[...]
    stacked = next(it) if first else q_ref
    rows = stacked.shape[0]
    chunk = chunk_of(rows)
    if first:
        for h in range(rows // tok):
            stacked[pl.ds(h * tok, tok), :] = q_ref[:, pl.ds(h * HD, HD)]
    keys = [r[0] for r in kv]
    vals = [r[1].T for r in kv]
    keys = keys[0] if blocks == 1 else jnp.concatenate(keys, axis=0)
    vals = vals[0] if blocks == 1 else jnp.concatenate(vals, axis=1)

    def scores(at):
        return lax.dot_general(
            keys, stacked[pl.ds(at, chunk), :], (((1,), (1,)), ((), ())), preferred_element_type=jnp.float32
        )

    ahead = scores(0)
    for at in range(0, rows, chunk):
        s = ahead * (LOG2E / math.sqrt(HD))
        if at + chunk < rows:
            ahead = scores(at + chunk)
        cols = pl.ds(at, chunk)
        top = jnp.max(s, axis=0, keepdims=True)
        if not first:
            old = m_in[:, cols]
            top = jnp.maximum(old, top)
            alpha = jnp.exp2(old - top)
        p = jnp.exp2(s - top)
        total = jnp.sum(p, axis=0, keepdims=True)
        out = jnp.dot(vals, p.astype(jnp.bfloat16), preferred_element_type=jnp.float32)
        if not first:
            total = total + alpha * l_in[:, cols]
            out = out + alpha * a_in[:, cols]
        if last:
            out = (out * (1.0 / total)).astype(o_ref.dtype).T
            done = at
            while done < at + chunk:
                h, t = divmod(done, tok)
                n = min(tok - t, at + chunk - done)
                o_ref[pl.ds(t, n), pl.ds(h * HD, HD)] = out[done - at : done - at + n]
                done += n
        else:
            m_out[:, cols] = top
            l_out[:, cols] = total
            a_out[:, cols] = out


def attend(queries, blocks, state=None, last=False, carry=None):
    tok = blocks[0].shape[1]
    rows = queries.size // HD
    if last:
        out_shape = (jax.ShapeDtypeStruct((tok, rows // tok * HD), queries.dtype),)
    else:
        out_shape = tuple(pltpu.VMEM((n, rows), jnp.float32) for n in (1, 1, HD))
    args = [queries, *blocks, *(state or ())]
    if carry is not None:
        args.append(carry)
        out_shape += (pltpu.VMEM(carry.shape, carry.dtype),)
    if state is None:
        out_shape += (pltpu.VMEM((rows, HD), queries.dtype),)
    else:
        args = [pltpu.with_memory_space_constraint(a, pltpu.VMEM) for a in args]
    pairs = rows * sum(b.shape[1] for b in blocks)
    return pl.pallas_call(
        functools.partial(attend_body, len(blocks), state is None, last, carry is not None),
        out_shape=out_shape,
        in_specs=[VMEM] * len(args),
        out_specs=(VMEM,) * len(out_shape),
        compiler_params=pltpu.CompilerParams(vmem_limit_bytes=24 << 20),
        cost_estimate=pl.CostEstimate(flops=4 * pairs * HD, bytes_accessed=0, transcendentals=pairs),
    )(*args)


def on_device(queries, keyval):
    count = lax.axis_size(AXIS)
    levels = count.bit_length() - 1
    me = lax.axis_index(AXIS)
    far = 3 << levels - 2

    def swap(value, bit):
        return lax.ppermute(value, AXIS, [(i, i ^ 1 << bit) for i in range(count)])

    def send(value, real):
        return lax.ppermute(value, AXIS, fill(real, count))

    received = {}
    *state, own, queries = attend(queries, [keyval], carry=keyval)
    first = own
    informed = [0, 1]
    for bit in [*range(1, levels - 1), None, levels - 1]:
        if bit is None:
            got, holder = send(keyval, [(0, far)]), far
        else:
            got, holder = swap(keyval, bit), 1 << bit
            received[bit] = got
        informed.append(holder)
        first = jnp.where(me == holder, got, first)
    received[0] = swap(own, 0)
    arrived = [received[bit] for bit in reversed(range(levels))]
    waves = plan(informed, count)
    for k, wave in enumerate(waves):
        came = [(send(first, real), [t for _, t in real]) for real in wave]
        if k + 1 == len(waves):
            *state, first = attend(queries, arrived, state, carry=first)
        for got, holders in came:
            first = jnp.where(member(me, holders), got, first)
    first = jnp.where(me % 2 == 1, swap(first, 0), first)
    return attend(queries, [first], state, last=True)[0]


def solution(mesh):
    return jax.shard_map(
        on_device,
        mesh=mesh,
        in_specs=(P(AXIS, None), P(None, AXIS, None)),
        out_specs=P(AXIS, None),
        check_vma=False,
    )
```

```python
import functools
import math

import jax
import jax.numpy as jnp
from jax import lax
from jax.experimental import pallas as pl
from jax.experimental.pallas import tpu as pltpu
from jax.sharding import PartitionSpec as P

HD = 128
AXIS = "seq"
FANOUT = 3
CHUNK = 512
LAST_CHUNK = 768
LOG2E = math.log2(math.e)
VMEM = pl.BlockSpec(memory_space=pltpu.VMEM)
TINY = pl.CostEstimate(flops=1, bytes_accessed=1, transcendentals=0)


def hops(a, b):
    return (a ^ b).bit_count()


def fill(real, count):
    goes = dict(real)
    open_to = set(range(count)) - set(goes.values())
    late = []
    for i in range(count):
        if i in goes:
            continue
        if i ^ 1 in open_to:
            goes[i] = i ^ 1
            open_to.remove(i ^ 1)
        else:
            late.append(i)
    for i in late:
        goes[i] = min(sorted(open_to), key=lambda t: (t == i, hops(t, i), t))
        open_to.remove(goes[i])
    for i in range(count):
        if goes[i] == i:
            goes[i], goes[i ^ 1] = goes[i ^ 1], goes[i]
    return sorted(goes.items())


def plan(seeds, later, count):
    slots = {s: list(range(FANOUT)) for s in seeds} | {s: [FANOUT - 1] for s in later}
    holders = {0, *slots} | {1 << b for b in range(count.bit_length() - 1)}
    missing = [t for t in range(0, count, 2) if t not in holders]
    waves = []
    while missing:
        wave = [[] for _ in range(FANOUT)]
        for t in sorted(missing, key=lambda t: (-min(hops(s, t) for s in slots), -t)):
            free = [s for s in slots if slots[s]]
            if not free:
                break
            s = min(free, key=lambda s: (hops(s, t), -s))
            wave[slots[s].pop(0)].append((s, t))
        waves.append([w for w in wave if w])
        holders |= {t for w in wave for _, t in w}
        slots = {s: list(range(FANOUT)) for s in holders}
        missing = [t for t in missing if t not in holders]
    return waves


def member(me, devices):
    hit = me == devices[0]
    for d in devices[1:]:
        hit = hit | (me == d)
    return hit


def chunk_of(rows, limit):
    return max(c for c in range(HD, rows + 1, HD) if rows % c == 0 and (c <= limit or c == HD))


def attend_body(blocks, first, last, carried, *refs):
    it = iter(refs)
    q_ref = next(it)
    kv = [next(it) for _ in range(blocks)]
    tok = kv[0].shape[1]
    if not first:
        m_in, l_in, a_in = next(it), next(it), next(it)
    if carried:
        carry_in = next(it)
    if last:
        o_ref = next(it)
    else:
        m_out, l_out, a_out = next(it), next(it), next(it)
    if carried:
        carry_out = next(it)
        carry_out[...] = carry_in[...]
    stacked = next(it) if first else q_ref
    rows = stacked.shape[0]
    chunk = chunk_of(rows, LAST_CHUNK if last else CHUNK)
    if first:
        for h in range(rows // tok):
            stacked[pl.ds(h * tok, tok), :] = q_ref[:, pl.ds(h * HD, HD)]
    keys = [r[0] for r in kv]
    vals = [r[1].T for r in kv]
    keys = keys[0] if blocks == 1 else jnp.concatenate(keys, axis=0)
    vals = vals[0] if blocks == 1 else jnp.concatenate(vals, axis=1)

    def scores(at):
        return lax.dot_general(
            keys, stacked[pl.ds(at, chunk), :], (((1,), (1,)), ((), ())), preferred_element_type=jnp.float32
        )

    ahead = scores(0)
    for at in range(0, rows, chunk):
        s = ahead * (LOG2E / math.sqrt(HD))
        if at + chunk < rows:
            ahead = scores(at + chunk)
        cols = pl.ds(at, chunk)
        top = jnp.max(s, axis=0, keepdims=True)
        if not first:
            old = m_in[:, cols]
            top = jnp.maximum(old, top)
            alpha = jnp.exp2(old - top)
        p = jnp.exp2(s - top)
        total = jnp.sum(p, axis=0, keepdims=True)
        out = jnp.dot(vals, p.astype(jnp.bfloat16), preferred_element_type=jnp.float32)
        if not first:
            total = total + alpha * l_in[:, cols]
            out = out + alpha * a_in[:, cols]
        if last:
            out = (out * (1.0 / total)).astype(o_ref.dtype).T
            done = at
            while done < at + chunk:
                h, t = divmod(done, tok)
                n = min(tok - t, at + chunk - done)
                o_ref[pl.ds(t, n), pl.ds(h * HD, HD)] = out[done - at : done - at + n]
                done += n
        else:
            m_out[:, cols] = top
            l_out[:, cols] = total
            a_out[:, cols] = out


def attend(queries, blocks, state=None, last=False, carry=None):
    tok = blocks[0].shape[1]
    rows = queries.size // HD
    if last:
        out_shape = (jax.ShapeDtypeStruct((tok, rows // tok * HD), queries.dtype),)
    else:
        out_shape = tuple(pltpu.VMEM((n, rows), jnp.float32) for n in (1, 1, HD))
    args = [queries, *blocks, *(state or ())]
    if carry is not None:
        args.append(carry)
        out_shape += (pltpu.VMEM(carry.shape, carry.dtype),)
    if state is None:
        out_shape += (pltpu.VMEM((rows, HD), queries.dtype),)
    args = [pltpu.with_memory_space_constraint(a, pltpu.VMEM) for a in args]
    pairs = rows * sum(b.shape[1] for b in blocks)
    return pl.pallas_call(
        functools.partial(attend_body, len(blocks), state is None, last, carry is not None),
        out_shape=out_shape,
        in_specs=[VMEM] * len(args),
        out_specs=(VMEM,) * len(out_shape),
        compiler_params=pltpu.CompilerParams(vmem_limit_bytes=24 << 20),
        cost_estimate=pl.CostEstimate(flops=4 * pairs * HD, bytes_accessed=0, transcendentals=pairs),
    )(*args)


def hold_body(block_ref, after_ref, out_ref):
    out_ref[...] = block_ref[...]


def hold(block, after):
    args = [pltpu.with_memory_space_constraint(a, pltpu.VMEM) for a in (block, after)]
    return pl.pallas_call(
        hold_body,
        out_shape=pltpu.VMEM(block.shape, block.dtype),
        in_specs=[VMEM, pl.BlockSpec(memory_space=pl.ANY)],
        out_specs=VMEM,
        cost_estimate=TINY,
    )(*args)


def pick_body(holders, *refs):
    *blocks, out_ref = refs
    me = lax.axis_index(AXIS)
    for block, holder in zip(blocks, holders):

        @pl.when(me == holder)
        def _():
            out_ref[...] = block[...]


def pick(blocks):
    args = [pltpu.with_memory_space_constraint(b, pltpu.VMEM) for b in blocks.values()]
    return pl.pallas_call(
        functools.partial(pick_body, tuple(blocks)),
        out_shape=pltpu.VMEM(args[0].shape, args[0].dtype),
        in_specs=[VMEM] * len(args),
        out_specs=VMEM,
        cost_estimate=TINY,
    )(*args)


def on_device(queries, keyval):
    count = lax.axis_size(AXIS)
    levels = count.bit_length() - 1
    me = lax.axis_index(AXIS)
    high, top = 1 << levels - 2, 1 << levels - 1

    def swap(value, bit):
        return lax.ppermute(value, AXIS, [(i, i ^ 1 << bit) for i in range(count)])

    def send(value, real):
        return lax.ppermute(value, AXIS, fill(real, count))

    received = {bit: swap(keyval, bit) for bit in range(1, levels)}
    seeds = {high: received[levels - 2]}
    seeds |= {holder: send(keyval, [(0, holder)]) for holder in (high | top, top)}
    first = pick(seeds)
    own = hold(keyval, first)
    later = {4: received[2]}
    waves = plan(list(seeds), list(later), count)
    for k, wave in enumerate(waves):
        came = []
        for real in wave:
            if k == 0 and real is wave[-1]:
                for holder, got in (later | {0: own}).items():
                    first = jnp.where(me == holder, got, first)
            came.append((send(first, real), [t for _, t in real]))
        if k == 0:
            for bit in range(1, levels - 2):
                if 1 << bit not in later:
                    first = jnp.where(me == 1 << bit, received[bit], first)
            received[0] = jnp.where(me == top, seeds[high | top], seeds[top])
            received[0] = jnp.where(me == 1, came[-1][0], received[0])
        if k + 1 == len(waves):
            *state, stacked = attend(queries, [own, *(received[bit] for bit in range(levels - 2, 0, -1))])
            *state, first = attend(stacked, [received[levels - 1]], state, carry=first)
        for got, holders in came:
            first = jnp.where(member(me, holders), got, first)
    passed = swap(first, 0)
    state = attend(stacked, [received[0]], state)
    first = jnp.where(me % 2 == 1, passed, first)
    return attend(stacked, [first], state, last=True)[0]


def solution(mesh):
    return jax.shard_map(
        on_device,
        mesh=mesh,
        in_specs=(P(AXIS, None), P(None, AXIS, None)),
        out_specs=P(AXIS, None),
        check_vma=False,
    )
```

```python
import functools
import math

import jax
import jax.numpy as jnp
from jax import lax
from jax.experimental import pallas as pl
from jax.experimental.pallas import tpu as pltpu
from jax.sharding import PartitionSpec as P

HD = 128
AXIS = "seq"
FANOUT = 3
CHUNK = 512
LAST_CHUNK = 768
LOG2E = math.log2(math.e)
VMEM = pl.BlockSpec(memory_space=pltpu.VMEM)
TINY = pl.CostEstimate(flops=1, bytes_accessed=1, transcendentals=0)


def hops(a, b):
    return (a ^ b).bit_count()


def fill(real, count):
    goes = dict(real)
    open_to = set(range(count)) - set(goes.values())
    late = []
    for i in range(count):
        if i in goes:
            continue
        if i ^ 1 in open_to:
            goes[i] = i ^ 1
            open_to.remove(i ^ 1)
        else:
            late.append(i)
    for i in late:
        goes[i] = min(sorted(open_to), key=lambda t: (t == i, hops(t, i), t))
        open_to.remove(goes[i])
    for i in range(count):
        if goes[i] == i:
            goes[i], goes[i ^ 1] = goes[i ^ 1], goes[i]
    return sorted(goes.items())


def plan(seeds, later, count):
    slots = {s: list(range(FANOUT)) for s in seeds} | {s: [FANOUT - 1] for s in later}
    holders = {0, *slots} | {1 << b for b in range(1, count.bit_length() - 1)}
    missing = [t for t in range(0, count, 2) if t not in holders]
    waves = []
    while missing:
        wave = [[] for _ in range(FANOUT)]
        for t in sorted(missing, key=lambda t: (-min(hops(s, t) for s in slots), -t)):
            free = [s for s in slots if slots[s]]
            if not free:
                break
            s = min(free, key=lambda s: (hops(s, t), -s))
            wave[slots[s].pop(0)].append((s, t))
        waves.append([w for w in wave if w])
        holders |= {t for w in wave for _, t in w}
        slots = {s: list(range(FANOUT)) for s in holders}
        missing = [t for t in missing if t not in holders]
    return waves


def member(me, devices):
    hit = me == devices[0]
    for d in devices[1:]:
        hit = hit | (me == d)
    return hit


def chunk_of(rows, limit):
    return max(c for c in range(HD, rows + 1, HD) if rows % c == 0 and (c <= limit or c == HD))


def attend_body(blocks, first, last, carried, *refs):
    it = iter(refs)
    q_ref = next(it)
    kv = [next(it) for _ in range(blocks)]
    tok = kv[0].shape[1]
    if not first:
        m_in, l_in, a_in = next(it), next(it), next(it)
    if carried:
        carry_in = next(it)
    if last:
        o_ref = next(it)
    else:
        m_out, l_out, a_out = next(it), next(it), next(it)
    if carried:
        carry_out = next(it)
        carry_out[...] = carry_in[...]
    stacked = next(it) if first else q_ref
    rows = stacked.shape[0]
    chunk = chunk_of(rows, LAST_CHUNK if last else CHUNK)
    if first:
        for h in range(rows // tok):
            stacked[pl.ds(h * tok, tok), :] = q_ref[:, pl.ds(h * HD, HD)]
    keys = [r[0] for r in kv]
    vals = [r[1].T for r in kv]
    keys = keys[0] if blocks == 1 else jnp.concatenate(keys, axis=0)
    vals = vals[0] if blocks == 1 else jnp.concatenate(vals, axis=1)

    def scores(at):
        return lax.dot_general(
            keys, stacked[pl.ds(at, chunk), :], (((1,), (1,)), ((), ())), preferred_element_type=jnp.float32
        )

    ahead = scores(0)
    for at in range(0, rows, chunk):
        s = ahead * (LOG2E / math.sqrt(HD))
        if at + chunk < rows:
            ahead = scores(at + chunk)
        cols = pl.ds(at, chunk)
        top = jnp.max(s, axis=0, keepdims=True)
        if not first:
            old = m_in[:, cols]
            top = jnp.maximum(old, top)
            alpha = jnp.exp2(old - top)
        p = jnp.exp2(s - top)
        total = jnp.sum(p, axis=0, keepdims=True)
        out = jnp.dot(vals, p.astype(jnp.bfloat16), preferred_element_type=jnp.float32)
        if not first:
            total = total + alpha * l_in[:, cols]
            out = out + alpha * a_in[:, cols]
        if last:
            out = (out * (1.0 / total)).astype(o_ref.dtype).T
            done = at
            while done < at + chunk:
                h, t = divmod(done, tok)
                n = min(tok - t, at + chunk - done)
                o_ref[pl.ds(t, n), pl.ds(h * HD, HD)] = out[done - at : done - at + n]
                done += n
        else:
            m_out[:, cols] = top
            l_out[:, cols] = total
            a_out[:, cols] = out


def attend(queries, blocks, state=None, last=False, carry=None):
    tok = blocks[0].shape[1]
    rows = queries.size // HD
    if last:
        out_shape = (jax.ShapeDtypeStruct((tok, rows // tok * HD), queries.dtype),)
    else:
        out_shape = tuple(pltpu.VMEM((n, rows), jnp.float32) for n in (1, 1, HD))
    args = [queries, *blocks, *(state or ())]
    if carry is not None:
        args.append(carry)
        out_shape += (pltpu.VMEM(carry.shape, carry.dtype),)
    if state is None:
        out_shape += (pltpu.VMEM((rows, HD), queries.dtype),)
    args = [pltpu.with_memory_space_constraint(a, pltpu.VMEM) for a in args]
    pairs = rows * sum(b.shape[1] for b in blocks)
    return pl.pallas_call(
        functools.partial(attend_body, len(blocks), state is None, last, carry is not None),
        out_shape=out_shape,
        in_specs=[VMEM] * len(args),
        out_specs=(VMEM,) * len(out_shape),
        compiler_params=pltpu.CompilerParams(vmem_limit_bytes=24 << 20),
        cost_estimate=pl.CostEstimate(flops=4 * pairs * HD, bytes_accessed=0, transcendentals=pairs),
    )(*args)


def hold_body(block_ref, after_ref, out_ref):
    out_ref[...] = block_ref[...]


def hold(block, after):
    args = [pltpu.with_memory_space_constraint(a, pltpu.VMEM) for a in (block, after)]
    return pl.pallas_call(
        hold_body,
        out_shape=pltpu.VMEM(block.shape, block.dtype),
        in_specs=[VMEM, pl.BlockSpec(memory_space=pl.ANY)],
        out_specs=VMEM,
        cost_estimate=TINY,
    )(*args)


def pick_body(holders, *refs):
    *blocks, out_ref = refs
    me = lax.axis_index(AXIS)
    for block, holder in zip(blocks, holders):

        @pl.when(me == holder)
        def _():
            out_ref[...] = block[...]


def pick(blocks):
    args = [pltpu.with_memory_space_constraint(b, pltpu.VMEM) for b in blocks.values()]
    return pl.pallas_call(
        functools.partial(pick_body, tuple(blocks)),
        out_shape=pltpu.VMEM(args[0].shape, args[0].dtype),
        in_specs=[VMEM] * len(args),
        out_specs=VMEM,
        cost_estimate=TINY,
    )(*args)


def on_device(queries, keyval):
    count = lax.axis_size(AXIS)
    levels = count.bit_length() - 1
    me = lax.axis_index(AXIS)
    high, top = 1 << levels - 2, 1 << levels - 1

    def swap(value, bit):
        return lax.ppermute(value, AXIS, [(i, i ^ 1 << bit) for i in range(count)])

    def send(value, real):
        return lax.ppermute(value, AXIS, fill(real, count))

    received = {bit: swap(keyval, bit) for bit in range(1, levels)}
    seeds = {holder: send(keyval, [(0, holder)]) for holder in (top, high | top)}
    seeds = {top: seeds[top], high: received[levels - 2], high | top: seeds[high | top]}
    first = pick(seeds)
    own = hold(keyval, first)
    later = {4: received[2]}
    waves = plan(list(seeds), list(later), count)
    for k, wave in enumerate(waves):
        filled = first
        if k == 0:
            for holder, got in (later | {0: own}).items():
                filled = jnp.where(me == holder, got, filled)
        came = [(send(filled, wave[-1]), [t for _, t in wave[-1]])]
        came += [(send(first, real), [t for _, t in real]) for real in wave[-2::-1]]
        first = filled
        if k == 0:
            for bit in range(1, levels - 2):
                if 1 << bit not in later:
                    first = jnp.where(me == 1 << bit, received[bit], first)
            received[0] = jnp.where(me == top, seeds[high | top], seeds[top])
            received[0] = jnp.where(me == 1, came[0][0], received[0])
        if k + 1 == len(waves):
            *state, stacked = attend(queries, [own, *(received[bit] for bit in range(levels - 2, 1, -1))])
            *state, first = attend(stacked, [received[1]], state, carry=first)
            first = hold(first, received[levels - 1])
        for got, holders in came:
            first = jnp.where(member(me, holders), got, first)
    passed = swap(first, 0)
    state = attend(stacked, [received[levels - 1], received[0]], state)
    first = jnp.where(me % 2 == 1, passed, first)
    return attend(stacked, [first], state, last=True)[0]


def solution(mesh):
    return jax.shard_map(
        on_device,
        mesh=mesh,
        in_specs=(P(AXIS, None), P(None, AXIS, None)),
        out_specs=P(AXIS, None),
        check_vma=False,
    )
```

```python
import functools
import math

import jax
import jax.numpy as jnp
from jax import lax
from jax.experimental import pallas as pl
from jax.experimental.pallas import tpu as pltpu
from jax.sharding import PartitionSpec as P

HD = 128
AXIS = "seq"
FANOUT = 3
CHUNK = 512
LAST_CHUNK = 768
LOG2E = math.log2(math.e)
VMEM = pl.BlockSpec(memory_space=pltpu.VMEM)
TINY = pl.CostEstimate(flops=1, bytes_accessed=1, transcendentals=0)


def hops(a, b):
    return (a ^ b).bit_count()


def fill(real, count):
    goes = dict(real)
    open_to = set(range(count)) - set(goes.values())
    late = []
    for i in range(count):
        if i in goes:
            continue
        if i ^ 1 in open_to:
            goes[i] = i ^ 1
            open_to.remove(i ^ 1)
        else:
            late.append(i)
    for i in late:
        goes[i] = min(sorted(open_to), key=lambda t: (t == i, hops(t, i), t))
        open_to.remove(goes[i])
    for i in range(count):
        if goes[i] == i:
            goes[i], goes[i ^ 1] = goes[i ^ 1], goes[i]
    return sorted(goes.items())


def plan(seeds, later, count):
    slots = {s: list(range(FANOUT)) for s in seeds} | {s: [FANOUT - 1] for s in later}
    holders = {0, *slots} | {1 << b for b in range(1, count.bit_length() - 1)}
    missing = [t for t in range(0, count, 2) if t not in holders]
    waves = []
    while missing:
        wave = [[] for _ in range(FANOUT)]
        for t in sorted(missing, key=lambda t: (-min(hops(s, t) for s in slots), -t)):
            free = [s for s in slots if slots[s]]
            if not free:
                break
            s = min(free, key=lambda s: (hops(s, t), -s))
            wave[slots[s].pop(0)].append((s, t))
        waves.append([w for w in wave if w])
        holders |= {t for w in wave for _, t in w}
        slots = {s: list(range(FANOUT)) for s in holders}
        missing = [t for t in missing if t not in holders]
    return waves


def member(me, devices):
    hit = me == devices[0]
    for d in devices[1:]:
        hit = hit | (me == d)
    return hit


def chunk_of(rows, limit):
    return max(c for c in range(HD, rows + 1, HD) if rows % c == 0 and (c <= limit or c == HD))


def attend_body(blocks, first, last, carried, *refs):
    it = iter(refs)
    q_ref = next(it)
    kv = [next(it) for _ in range(blocks)]
    tok = kv[0].shape[1]
    if not first:
        m_in, l_in, a_in = next(it), next(it), next(it)
    if carried:
        carry_in = next(it)
    if last:
        o_ref = next(it)
    else:
        m_out, l_out, a_out = next(it), next(it), next(it)
    if carried:
        carry_out = next(it)
        carry_out[...] = carry_in[...]
    stacked = next(it) if first else q_ref
    rows = stacked.shape[0]
    chunk = chunk_of(rows, LAST_CHUNK if last else CHUNK)
    if first:
        for h in range(rows // tok):
            stacked[pl.ds(h * tok, tok), :] = q_ref[:, pl.ds(h * HD, HD)]
    keys = [r[0] for r in kv]
    vals = [r[1].T for r in kv]
    keys = keys[0] if blocks == 1 else jnp.concatenate(keys, axis=0)
    vals = vals[0] if blocks == 1 else jnp.concatenate(vals, axis=1)

    def scores(at):
        return lax.dot_general(
            keys, stacked[pl.ds(at, chunk), :], (((1,), (1,)), ((), ())), preferred_element_type=jnp.float32
        )

    ahead = scores(0)
    for at in range(0, rows, chunk):
        s = ahead * (LOG2E / math.sqrt(HD))
        if at + chunk < rows:
            ahead = scores(at + chunk)
        cols = pl.ds(at, chunk)
        top = jnp.max(s, axis=0, keepdims=True)
        if not first:
            old = m_in[:, cols]
            top = jnp.maximum(old, top)
            alpha = jnp.exp2(old - top)
        p = jnp.exp2(s - top)
        total = jnp.sum(p, axis=0, keepdims=True)
        out = jnp.dot(vals, p.astype(jnp.bfloat16), preferred_element_type=jnp.float32)
        if not first:
            total = total + alpha * l_in[:, cols]
            out = out + alpha * a_in[:, cols]
        if last:
            out = (out * (1.0 / total)).astype(o_ref.dtype).T
            done = at
            while done < at + chunk:
                h, t = divmod(done, tok)
                n = min(tok - t, at + chunk - done)
                o_ref[pl.ds(t, n), pl.ds(h * HD, HD)] = out[done - at : done - at + n]
                done += n
        else:
            m_out[:, cols] = top
            l_out[:, cols] = total
            a_out[:, cols] = out


def attend(queries, blocks, state=None, last=False, carry=None):
    tok = blocks[0].shape[1]
    rows = queries.size // HD
    if last:
        out_shape = (jax.ShapeDtypeStruct((tok, rows // tok * HD), queries.dtype),)
    else:
        out_shape = tuple(pltpu.VMEM((n, rows), jnp.float32) for n in (1, 1, HD))
    args = [queries, *blocks, *(state or ())]
    if carry is not None:
        args.append(carry)
        out_shape += (pltpu.VMEM(carry.shape, carry.dtype),)
    if state is None:
        out_shape += (pltpu.VMEM((rows, HD), queries.dtype),)
    args = [pltpu.with_memory_space_constraint(a, pltpu.VMEM) for a in args]
    pairs = rows * sum(b.shape[1] for b in blocks)
    return pl.pallas_call(
        functools.partial(attend_body, len(blocks), state is None, last, carry is not None),
        out_shape=out_shape,
        in_specs=[VMEM] * len(args),
        out_specs=(VMEM,) * len(out_shape),
        compiler_params=pltpu.CompilerParams(vmem_limit_bytes=24 << 20),
        cost_estimate=pl.CostEstimate(flops=40 * pairs * HD, bytes_accessed=0, transcendentals=pairs),
    )(*args)


def hold_body(block_ref, after_ref, out_ref):
    out_ref[...] = block_ref[...]


def hold(block, after):
    args = [pltpu.with_memory_space_constraint(a, pltpu.VMEM) for a in (block, after)]
    return pl.pallas_call(
        hold_body,
        out_shape=pltpu.VMEM(block.shape, block.dtype),
        in_specs=[VMEM, pl.BlockSpec(memory_space=pl.ANY)],
        out_specs=VMEM,
        cost_estimate=TINY,
    )(*args)


def pick_body(holders, *refs):
    *blocks, out_ref = refs
    me = lax.axis_index(AXIS)
    for block, holder in zip(blocks, holders):

        @pl.when(me == holder)
        def _():
            out_ref[...] = block[...]


def pick(blocks):
    args = [pltpu.with_memory_space_constraint(b, pltpu.VMEM) for b in blocks.values()]
    return pl.pallas_call(
        functools.partial(pick_body, tuple(blocks)),
        out_shape=pltpu.VMEM(args[0].shape, args[0].dtype),
        in_specs=[VMEM] * len(args),
        out_specs=VMEM,
        cost_estimate=TINY,
    )(*args)


def on_device(queries, keyval):
    count = lax.axis_size(AXIS)
    levels = count.bit_length() - 1
    me = lax.axis_index(AXIS)
    high, top = 1 << levels - 2, 1 << levels - 1

    def swap(value, bit):
        return lax.ppermute(value, AXIS, [(i, i ^ 1 << bit) for i in range(count)])

    def send(value, real):
        return lax.ppermute(value, AXIS, fill(real, count))

    received = {bit: swap(keyval, bit) for bit in range(1, levels)}
    seeds = {holder: send(keyval, [(0, holder)]) for holder in (top, high | top)}
    seeds = {top: seeds[top], high: received[levels - 2], high | top: seeds[high | top]}
    first = pick(seeds)
    own = hold(keyval, first)
    later = {4: received[2]}
    waves = plan(list(seeds), list(later), count)
    for k, wave in enumerate(waves):
        filled = first
        if k == 0:
            for holder, got in (later | {0: own}).items():
                filled = jnp.where(me == holder, got, filled)
        came = [(send(filled, wave[-1]), [t for _, t in wave[-1]])]
        came += [(send(first, real), [t for _, t in real]) for real in wave[-2::-1]]
        first = filled
        if k == 0:
            for bit in range(1, levels - 2):
                if 1 << bit not in later:
                    first = jnp.where(me == 1 << bit, received[bit], first)
            received[0] = jnp.where(me == top, seeds[high | top], seeds[top])
            received[0] = jnp.where(me == 1, came[0][0], received[0])
        if k + 1 == len(waves):
            *state, stacked = attend(queries, [own, *(received[bit] for bit in range(levels - 2, 1, -1))])
            *state, first = attend(stacked, [received[1]], state, carry=first)
            first = hold(first, received[levels - 1])
        for got, holders in came:
            first = jnp.where(member(me, holders), got, first)
    passed = swap(first, 0)
    state = attend(stacked, [received[levels - 1], received[0]], state)
    first = jnp.where(me % 2 == 1, passed, first)
    return attend(stacked, [first], state, last=True)[0]


def solution(mesh):
    return jax.shard_map(
        on_device,
        mesh=mesh,
        in_specs=(P(AXIS, None), P(None, AXIS, None)),
        out_specs=P(AXIS, None),
        check_vma=False,
    )
```

```python
import functools
import math

import jax
import jax.numpy as jnp
from jax import lax
from jax.experimental import pallas as pl
from jax.experimental.pallas import tpu as pltpu
from jax.sharding import PartitionSpec as P

HD = 128
AXIS = "seq"
FANOUT = 3
CHUNK = 512
LAST_CHUNK = 768
LOG2E = math.log2(math.e)
VMEM = pl.BlockSpec(memory_space=pltpu.VMEM)
TINY = pl.CostEstimate(flops=1, bytes_accessed=1, transcendentals=0)


def hops(a, b):
    return (a ^ b).bit_count()


def fill(real, count):
    goes = dict(real)
    open_to = set(range(count)) - set(goes.values())
    late = []
    for i in range(count):
        if i in goes:
            continue
        if i ^ 1 in open_to:
            goes[i] = i ^ 1
            open_to.remove(i ^ 1)
        else:
            late.append(i)
    for i in late:
        goes[i] = min(sorted(open_to), key=lambda t: (t == i, hops(t, i), t))
        open_to.remove(goes[i])
    for i in range(count):
        if goes[i] == i:
            goes[i], goes[i ^ 1] = goes[i ^ 1], goes[i]
    return sorted(goes.items())


def plan(seeds, later, count):
    slots = {s: list(range(FANOUT)) for s in seeds} | {s: [FANOUT - 1] for s in later}
    holders = {0, *slots} | {1 << b for b in range(1, count.bit_length() - 1)}
    missing = [t for t in range(0, count, 2) if t not in holders]
    waves = []
    while missing:
        wave = [[] for _ in range(FANOUT)]
        for t in sorted(missing, key=lambda t: (-min(hops(s, t) for s in slots), -t)):
            free = [s for s in slots if slots[s]]
            if not free:
                break
            s = min(free, key=lambda s: (hops(s, t), -s))
            wave[slots[s].pop(0)].append((s, t))
        waves.append([w for w in wave if w])
        holders |= {t for w in wave for _, t in w}
        slots = {s: list(range(FANOUT)) for s in holders}
        missing = [t for t in missing if t not in holders]
    return waves


def member(me, devices):
    hit = me == devices[0]
    for d in devices[1:]:
        hit = hit | (me == d)
    return hit


def chunk_of(rows, limit):
    return max(c for c in range(HD, rows + 1, HD) if rows % c == 0 and (c <= limit or c == HD))


def attend_body(blocks, first, last, carried, *refs):
    it = iter(refs)
    q_ref = next(it)
    kv = [next(it) for _ in range(blocks)]
    tok = kv[0].shape[1]
    if not first:
        m_in, l_in, a_in = next(it), next(it), next(it)
    if carried:
        carry_in = next(it)
    if last:
        o_ref = next(it)
    else:
        m_out, l_out, a_out = next(it), next(it), next(it)
    if carried:
        carry_out = next(it)
        carry_out[...] = carry_in[...]
    stacked = next(it) if first else q_ref
    rows = stacked.shape[0]
    chunk = chunk_of(rows, LAST_CHUNK if last else CHUNK)
    if first:
        for h in range(rows // tok):
            stacked[pl.ds(h * tok, tok), :] = q_ref[:, pl.ds(h * HD, HD)]
    keys = [r[0] for r in kv]
    vals = [r[1].T for r in kv]
    keys = keys[0] if blocks == 1 else jnp.concatenate(keys, axis=0)
    vals = vals[0] if blocks == 1 else jnp.concatenate(vals, axis=1)

    def scores(at):
        return lax.dot_general(
            keys, stacked[pl.ds(at, chunk), :], (((1,), (1,)), ((), ())), preferred_element_type=jnp.float32
        )

    ahead = scores(0)
    for at in range(0, rows, chunk):
        s = ahead * (LOG2E / math.sqrt(HD))
        if at + chunk < rows:
            ahead = scores(at + chunk)
        cols = pl.ds(at, chunk)
        top = jnp.max(s, axis=0, keepdims=True)
        if not first:
            old = m_in[:, cols]
            top = jnp.maximum(old, top)
            alpha = jnp.exp2(old - top)
        p = jnp.exp2(s - top)
        total = jnp.sum(p, axis=0, keepdims=True)
        out = jnp.dot(vals, p.astype(jnp.bfloat16), preferred_element_type=jnp.float32)
        if not first:
            total = total + alpha * l_in[:, cols]
            out = out + alpha * a_in[:, cols]
        if last:
            out = (out * (1.0 / total)).astype(o_ref.dtype).T
            done = at
            while done < at + chunk:
                h, t = divmod(done, tok)
                n = min(tok - t, at + chunk - done)
                o_ref[pl.ds(t, n), pl.ds(h * HD, HD)] = out[done - at : done - at + n]
                done += n
        else:
            m_out[:, cols] = top
            l_out[:, cols] = total
            a_out[:, cols] = out


def attend(queries, blocks, state=None, last=False, carry=None):
    tok = blocks[0].shape[1]
    rows = queries.size // HD
    if last:
        out_shape = (jax.ShapeDtypeStruct((tok, rows // tok * HD), queries.dtype),)
    else:
        out_shape = tuple(pltpu.VMEM((n, rows), jnp.float32) for n in (1, 1, HD))
    args = [queries, *blocks, *(state or ())]
    if carry is not None:
        args.append(carry)
        out_shape += (pltpu.VMEM(carry.shape, carry.dtype),)
    if state is None:
        out_shape += (pltpu.VMEM((rows, HD), queries.dtype),)
    args = [pltpu.with_memory_space_constraint(a, pltpu.VMEM) for a in args]
    pairs = rows * sum(b.shape[1] for b in blocks)
    return pl.pallas_call(
        functools.partial(attend_body, len(blocks), state is None, last, carry is not None),
        out_shape=out_shape,
        in_specs=[VMEM] * len(args),
        out_specs=(VMEM,) * len(out_shape),
        compiler_params=pltpu.CompilerParams(vmem_limit_bytes=24 << 20),
        cost_estimate=pl.CostEstimate(flops=40 * pairs * HD, bytes_accessed=0, transcendentals=pairs),
    )(*args)


def hold_body(block_ref, after_ref, out_ref):
    out_ref[...] = block_ref[...]


def hold(block, after):
    args = [pltpu.with_memory_space_constraint(a, pltpu.VMEM) for a in (block, after)]
    return pl.pallas_call(
        hold_body,
        out_shape=pltpu.VMEM(block.shape, block.dtype),
        in_specs=[VMEM, pl.BlockSpec(memory_space=pl.ANY)],
        out_specs=VMEM,
        cost_estimate=TINY,
    )(*args)


def pick_body(holders, *refs):
    *blocks, out_ref = refs
    me = lax.axis_index(AXIS)
    for block, holder in zip(blocks, holders):

        @pl.when(me == holder)
        def _():
            out_ref[...] = block[...]


def pick(blocks):
    args = [pltpu.with_memory_space_constraint(b, pltpu.VMEM) for b in blocks.values()]
    return pl.pallas_call(
        functools.partial(pick_body, tuple(blocks)),
        out_shape=pltpu.VMEM(args[0].shape, args[0].dtype),
        in_specs=[VMEM] * len(args),
        out_specs=VMEM,
        cost_estimate=TINY,
    )(*args)


def way(target, side):
    stops = [0, target, target ^ 1, target ^ side, target ^ side ^ 1, side ^ 1, side, 1, 0]
    return list(zip(stops, stops[1:]))


def on_device(queries, keyval):
    count = lax.axis_size(AXIS)
    levels = count.bit_length() - 1
    me = lax.axis_index(AXIS)
    high, top = 1 << levels - 2, 1 << levels - 1

    def swap(value, bit):
        return lax.ppermute(value, AXIS, [(i, i ^ 1 << bit) for i in range(count)])

    def send(value, real):
        return lax.ppermute(value, AXIS, fill(real, count))

    received = {bit: swap(keyval, bit) for bit in range(1, levels)}
    seeds = {holder: send(keyval, way(holder, side)) for holder, side in ((top, 4), (high | top, 2))}
    seeds = {top: seeds[top], high: received[levels - 2], high | top: seeds[high | top]}
    first = pick(seeds)
    own = hold(keyval, first)
    later = {4: received[2]}
    waves = plan(list(seeds), list(later), count)
    for k, wave in enumerate(waves):
        filled = first
        if k == 0:
            for holder, got in (later | {0: own}).items():
                filled = jnp.where(me == holder, got, filled)
        came = [(send(filled, wave[-1]), [t for _, t in wave[-1]])]
        came += [(send(first, real), [t for _, t in real]) for real in wave[-2::-1]]
        first = filled
        if k == 0:
            for bit in range(1, levels - 2):
                if 1 << bit not in later:
                    first = jnp.where(me == 1 << bit, received[bit], first)
            received[0] = jnp.where(member(me, [top, top ^ 4, 5]), seeds[high | top], seeds[top])
            received[0] = jnp.where(me == 1, came[0][0], received[0])
        if k + 1 == len(waves):
            *state, stacked = attend(queries, [own, *(received[bit] for bit in range(levels - 2, 1, -1))])
            *state, first = attend(stacked, [received[1]], state, carry=first)
            first = hold(first, received[levels - 1])
        for got, holders in came:
            first = jnp.where(member(me, holders), got, first)
    passed = swap(first, 0)
    state = attend(stacked, [received[levels - 1], received[0]], state)
    first = jnp.where(me % 2 == 1, passed, first)
    return attend(stacked, [first], state, last=True)[0]


def solution(mesh):
    return jax.shard_map(
        on_device,
        mesh=mesh,
        in_specs=(P(AXIS, None), P(None, AXIS, None)),
        out_specs=P(AXIS, None),
        check_vma=False,
    )
```

```python
import functools
import math

import jax
import jax.numpy as jnp
from jax import lax
from jax.experimental import pallas as pl
from jax.experimental.pallas import tpu as pltpu
from jax.sharding import PartitionSpec as P

HD = 128
AXIS = "seq"
FANOUT = 3
CHUNK = 512
LAST_CHUNK = 768
LOG2E = math.log2(math.e)
VMEM = pl.BlockSpec(memory_space=pltpu.VMEM)
TINY = pl.CostEstimate(flops=1, bytes_accessed=1, transcendentals=0)


def hops(a, b):
    return (a ^ b).bit_count()


def fill(real, count):
    goes = dict(real)
    open_to = set(range(count)) - set(goes.values())
    late = []
    for i in range(count):
        if i in goes:
            continue
        if i ^ 1 in open_to:
            goes[i] = i ^ 1
            open_to.remove(i ^ 1)
        else:
            late.append(i)
    for i in late:
        goes[i] = min(sorted(open_to), key=lambda t: (t == i, hops(t, i), t))
        open_to.remove(goes[i])
    for i in range(count):
        if goes[i] == i:
            goes[i], goes[i ^ 1] = goes[i ^ 1], goes[i]
    return sorted(goes.items())


def plan(seeds, later, count):
    slots = {s: list(range(FANOUT)) for s in seeds} | {s: [FANOUT - 1] for s in later}
    holders = {0, *slots} | {1 << b for b in range(1, count.bit_length() - 1)}
    missing = [t for t in range(0, count, 2) if t not in holders]
    waves = []
    while missing:
        wave = [[] for _ in range(FANOUT)]
        for t in sorted(missing, key=lambda t: (-min(hops(s, t) for s in slots), -t)):
            free = [s for s in slots if slots[s]]
            if not free:
                break
            s = min(free, key=lambda s: (hops(s, t), -s))
            wave[slots[s].pop(0)].append((s, t))
        waves.append([w for w in wave if w])
        holders |= {t for w in wave for _, t in w}
        slots = {s: list(range(FANOUT)) for s in holders}
        missing = [t for t in missing if t not in holders]
    return waves


def member(me, devices):
    hit = me == devices[0]
    for d in devices[1:]:
        hit = hit | (me == d)
    return hit


def chunk_of(rows, limit):
    return max(c for c in range(HD, rows + 1, HD) if rows % c == 0 and (c <= limit or c == HD))


def attend_body(blocks, first, last, carried, *refs):
    it = iter(refs)
    q_ref = next(it)
    kv = [next(it) for _ in range(blocks)]
    tok = kv[0].shape[1]
    if not first:
        m_in, l_in, a_in = next(it), next(it), next(it)
    if carried:
        carry_in = next(it)
    if last:
        o_ref = next(it)
    else:
        m_out, l_out, a_out = next(it), next(it), next(it)
    if carried:
        carry_out = next(it)
        carry_out[...] = carry_in[...]
    stacked = next(it) if first else q_ref
    rows = stacked.shape[0]
    chunk = chunk_of(rows, LAST_CHUNK if last else CHUNK)
    if first:
        for h in range(rows // tok):
            stacked[pl.ds(h * tok, tok), :] = q_ref[:, pl.ds(h * HD, HD)]
    keys = [r[0] for r in kv]
    vals = [r[1].T for r in kv]
    keys = keys[0] if blocks == 1 else jnp.concatenate(keys, axis=0)
    vals = vals[0] if blocks == 1 else jnp.concatenate(vals, axis=1)

    def scores(at):
        return lax.dot_general(
            keys, stacked[pl.ds(at, chunk), :], (((1,), (1,)), ((), ())), preferred_element_type=jnp.float32
        )

    ahead = scores(0)
    for at in range(0, rows, chunk):
        s = ahead * (LOG2E / math.sqrt(HD))
        if at + chunk < rows:
            ahead = scores(at + chunk)
        cols = pl.ds(at, chunk)
        top = jnp.max(s, axis=0, keepdims=True)
        if not first:
            old = m_in[:, cols]
            top = jnp.maximum(old, top)
            alpha = jnp.exp2(old - top)
        p = jnp.exp2(s - top)
        total = jnp.sum(p, axis=0, keepdims=True)
        out = jnp.dot(vals, p.astype(jnp.bfloat16), preferred_element_type=jnp.float32)
        if not first:
            total = total + alpha * l_in[:, cols]
            out = out + alpha * a_in[:, cols]
        if last:
            out = (out * (1.0 / total)).astype(o_ref.dtype).T
            done = at
            while done < at + chunk:
                h, t = divmod(done, tok)
                n = min(tok - t, at + chunk - done)
                o_ref[pl.ds(t, n), pl.ds(h * HD, HD)] = out[done - at : done - at + n]
                done += n
        else:
            m_out[:, cols] = top
            l_out[:, cols] = total
            a_out[:, cols] = out


def attend(queries, blocks, state=None, last=False, carry=None):
    tok = blocks[0].shape[1]
    rows = queries.size // HD
    if last:
        out_shape = (jax.ShapeDtypeStruct((tok, rows // tok * HD), queries.dtype),)
    else:
        out_shape = tuple(pltpu.VMEM((n, rows), jnp.float32) for n in (1, 1, HD))
    args = [queries, *blocks, *(state or ())]
    if carry is not None:
        args.append(carry)
        out_shape += (pltpu.VMEM(carry.shape, carry.dtype),)
    if state is None:
        out_shape += (pltpu.VMEM((rows, HD), queries.dtype),)
    args = [pltpu.with_memory_space_constraint(a, pltpu.VMEM) for a in args]
    pairs = rows * sum(b.shape[1] for b in blocks)
    return pl.pallas_call(
        functools.partial(attend_body, len(blocks), state is None, last, carry is not None),
        out_shape=out_shape,
        in_specs=[VMEM] * len(args),
        out_specs=(VMEM,) * len(out_shape),
        compiler_params=pltpu.CompilerParams(vmem_limit_bytes=24 << 20),
        cost_estimate=pl.CostEstimate(flops=40 * pairs * HD, bytes_accessed=0, transcendentals=pairs),
    )(*args)


def hold_body(block_ref, after_ref, out_ref):
    out_ref[...] = block_ref[...]


def hold(block, after):
    args = [pltpu.with_memory_space_constraint(a, pltpu.VMEM) for a in (block, after)]
    return pl.pallas_call(
        hold_body,
        out_shape=pltpu.VMEM(block.shape, block.dtype),
        in_specs=[VMEM, pl.BlockSpec(memory_space=pl.ANY)],
        out_specs=VMEM,
        cost_estimate=TINY,
    )(*args)


def pick_body(holders, *refs):
    *blocks, out_ref = refs
    me = lax.axis_index(AXIS)
    for block, holder in zip(blocks, holders):

        @pl.when(me == holder)
        def _():
            out_ref[...] = block[...]


def pick(blocks):
    args = [pltpu.with_memory_space_constraint(b, pltpu.VMEM) for b in blocks.values()]
    return pl.pallas_call(
        functools.partial(pick_body, tuple(blocks)),
        out_shape=pltpu.VMEM(args[0].shape, args[0].dtype),
        in_specs=[VMEM] * len(args),
        out_specs=VMEM,
        cost_estimate=TINY,
    )(*args)


def way(target, side):
    stops = [0, target, target ^ 1, target ^ side, target ^ side ^ 1, side ^ 1, side, 1, 0]
    return list(zip(stops, stops[1:]))


def on_device(queries, keyval):
    count = lax.axis_size(AXIS)
    levels = count.bit_length() - 1
    me = lax.axis_index(AXIS)
    high, top = 1 << levels - 2, 1 << levels - 1

    def swap(value, bit):
        return lax.ppermute(value, AXIS, [(i, i ^ 1 << bit) for i in range(count)])

    def send(value, real):
        return lax.ppermute(value, AXIS, fill(real, count))

    received = {bit: swap(keyval, bit) for bit in range(1, levels)}
    seeds = {holder: send(keyval, way(holder, side)) for holder, side in ((top, 4), (high | top, 2))}
    seeds = {top: seeds[top], high: received[levels - 2], high | top: seeds[high | top]}
    first = pick(seeds)
    own = hold(keyval, first)
    later = {4: received[2]}
    waves = plan(list(seeds), list(later), count)
    for k, wave in enumerate(waves):
        filled = first
        if k == 0:
            for holder, got in (later | {0: own}).items():
                filled = jnp.where(me == holder, got, filled)
        came = [(send(filled, wave[-1]), [t for _, t in wave[-1]])]
        came += [(send(first, real), [t for _, t in real]) for real in wave[:-1]]
        first = filled
        if k == 0:
            for bit in range(1, levels - 2):
                if 1 << bit not in later:
                    first = jnp.where(me == 1 << bit, received[bit], first)
            received[0] = jnp.where(member(me, [top, top ^ 4, 5]), seeds[high | top], seeds[top])
            received[0] = jnp.where(me == 1, came[0][0], received[0])
        if k + 1 == len(waves):
            *state, stacked = attend(queries, [own, *(received[bit] for bit in range(levels - 2, 1, -1))])
            *state, first = attend(stacked, [received[1]], state, carry=first)
            first = hold(first, received[levels - 1])
        for got, holders in came:
            first = jnp.where(member(me, holders), got, first)
    passed = swap(first, 0)
    state = attend(stacked, [received[levels - 1], received[0]], state)
    first = jnp.where(me % 2 == 1, passed, first)
    return attend(stacked, [first], state, last=True)[0]


def solution(mesh):
    return jax.shard_map(
        on_device,
        mesh=mesh,
        in_specs=(P(AXIS, None), P(None, AXIS, None)),
        out_specs=P(AXIS, None),
        check_vma=False,
    )
```

```python
import functools
import math

import jax
import jax.numpy as jnp
from jax import lax
from jax.experimental import pallas as pl
from jax.experimental.pallas import tpu as pltpu
from jax.sharding import PartitionSpec as P

HD = 128
AXIS = "seq"
FANOUT = 3
CHUNK = 768
LAST_CHUNK = 768
LOG2E = math.log2(math.e)
VMEM = pl.BlockSpec(memory_space=pltpu.VMEM)
TINY = pl.CostEstimate(flops=1, bytes_accessed=1, transcendentals=0)


def hops(a, b):
    return (a ^ b).bit_count()


def fill(real, count):
    goes = dict(real)
    open_to = set(range(count)) - set(goes.values())
    late = []
    for i in range(count):
        if i in goes:
            continue
        if i ^ 1 in open_to:
            goes[i] = i ^ 1
            open_to.remove(i ^ 1)
        else:
            late.append(i)
    for i in late:
        goes[i] = min(sorted(open_to), key=lambda t: (t == i, hops(t, i), t))
        open_to.remove(goes[i])
    for i in range(count):
        if goes[i] == i:
            goes[i], goes[i ^ 1] = goes[i ^ 1], goes[i]
    return sorted(goes.items())


def plan(seeds, later, count):
    slots = {s: list(range(FANOUT)) for s in seeds} | {s: [FANOUT - 1] for s in later}
    holders = {0, *slots} | {1 << b for b in range(1, count.bit_length() - 1)}
    missing = [t for t in range(0, count, 2) if t not in holders]
    waves = []
    while missing:
        wave = [[] for _ in range(FANOUT)]
        for t in sorted(missing, key=lambda t: (-min(hops(s, t) for s in slots), -t)):
            free = [s for s in slots if slots[s]]
            if not free:
                break
            s = min(free, key=lambda s: (hops(s, t), -s))
            wave[slots[s].pop(0)].append((s, t))
        waves.append([w for w in wave if w])
        holders |= {t for w in wave for _, t in w}
        slots = {s: list(range(FANOUT)) for s in holders}
        missing = [t for t in missing if t not in holders]
    return waves


def member(me, devices):
    hit = me == devices[0]
    for d in devices[1:]:
        hit = hit | (me == d)
    return hit


def chunk_of(rows, limit):
    return max(c for c in range(HD, rows + 1, HD) if rows % c == 0 and (c <= limit or c == HD))


def attend_body(blocks, first, last, carried, *refs):
    it = iter(refs)
    q_ref = next(it)
    kv = [next(it) for _ in range(blocks)]
    tok = kv[0].shape[1]
    if not first:
        m_in, l_in, a_in = next(it), next(it), next(it)
    if carried:
        carry_in = next(it)
    if last:
        o_ref = next(it)
    else:
        m_out, l_out, a_out = next(it), next(it), next(it)
    if carried:
        carry_out = next(it)
        carry_out[...] = carry_in[...]
    stacked = next(it) if first else q_ref
    rows = stacked.shape[0]
    chunk = chunk_of(rows, LAST_CHUNK if last else CHUNK)
    if first:
        for h in range(rows // tok):
            stacked[pl.ds(h * tok, tok), :] = q_ref[:, pl.ds(h * HD, HD)]
    keys = [r[0] for r in kv]
    vals = [r[1].T for r in kv]
    keys = keys[0] if blocks == 1 else jnp.concatenate(keys, axis=0)
    vals = vals[0] if blocks == 1 else jnp.concatenate(vals, axis=1)

    def scores(at):
        return lax.dot_general(
            keys, stacked[pl.ds(at, chunk), :], (((1,), (1,)), ((), ())), preferred_element_type=jnp.float32
        )

    ahead = scores(0)
    for at in range(0, rows, chunk):
        s = ahead * (LOG2E / math.sqrt(HD))
        if at + chunk < rows:
            ahead = scores(at + chunk)
        cols = pl.ds(at, chunk)
        top = jnp.max(s, axis=0, keepdims=True)
        if not first:
            old = m_in[:, cols]
            top = jnp.maximum(old, top)
            alpha = jnp.exp2(old - top)
        p = jnp.exp2(s - top)
        total = jnp.sum(p, axis=0, keepdims=True)
        out = jnp.dot(vals, p.astype(jnp.bfloat16), preferred_element_type=jnp.float32)
        if not first:
            total = total + alpha * l_in[:, cols]
            out = out + alpha * a_in[:, cols]
        if last:
            out = (out * (1.0 / total)).astype(o_ref.dtype).T
            done = at
            while done < at + chunk:
                h, t = divmod(done, tok)
                n = min(tok - t, at + chunk - done)
                o_ref[pl.ds(t, n), pl.ds(h * HD, HD)] = out[done - at : done - at + n]
                done += n
        else:
            m_out[:, cols] = top
            l_out[:, cols] = total
            a_out[:, cols] = out


def attend(queries, blocks, state=None, last=False, carry=None):
    tok = blocks[0].shape[1]
    rows = queries.size // HD
    if last:
        out_shape = (jax.ShapeDtypeStruct((tok, rows // tok * HD), queries.dtype),)
    else:
        out_shape = tuple(pltpu.VMEM((n, rows), jnp.float32) for n in (1, 1, HD))
    args = [queries, *blocks, *(state or ())]
    if carry is not None:
        args.append(carry)
        out_shape += (pltpu.VMEM(carry.shape, carry.dtype),)
    if state is None:
        out_shape += (pltpu.VMEM((rows, HD), queries.dtype),)
    args = [pltpu.with_memory_space_constraint(a, pltpu.VMEM) for a in args]
    pairs = rows * sum(b.shape[1] for b in blocks)
    return pl.pallas_call(
        functools.partial(attend_body, len(blocks), state is None, last, carry is not None),
        out_shape=out_shape,
        in_specs=[VMEM] * len(args),
        out_specs=(VMEM,) * len(out_shape),
        compiler_params=pltpu.CompilerParams(vmem_limit_bytes=24 << 20),
        cost_estimate=pl.CostEstimate(flops=40 * pairs * HD, bytes_accessed=0, transcendentals=pairs),
    )(*args)


def hold_body(block_ref, after_ref, out_ref):
    out_ref[...] = block_ref[...]


def hold(block, after):
    args = [pltpu.with_memory_space_constraint(a, pltpu.VMEM) for a in (block, after)]
    return pl.pallas_call(
        hold_body,
        out_shape=pltpu.VMEM(block.shape, block.dtype),
        in_specs=[VMEM, pl.BlockSpec(memory_space=pl.ANY)],
        out_specs=VMEM,
        cost_estimate=TINY,
    )(*args)


def pick_body(holders, *refs):
    *blocks, out_ref = refs
    me = lax.axis_index(AXIS)
    for block, holder in zip(blocks, holders):

        @pl.when(me == holder)
        def _():
            out_ref[...] = block[...]


def pick(blocks):
    args = [pltpu.with_memory_space_constraint(b, pltpu.VMEM) for b in blocks.values()]
    return pl.pallas_call(
        functools.partial(pick_body, tuple(blocks)),
        out_shape=pltpu.VMEM(args[0].shape, args[0].dtype),
        in_specs=[VMEM] * len(args),
        out_specs=VMEM,
        cost_estimate=TINY,
    )(*args)


def way(target, side):
    stops = [0, target, target ^ 1, target ^ side, target ^ side ^ 1, side ^ 1, side, 1, 0]
    return list(zip(stops, stops[1:]))


def on_device(queries, keyval):
    count = lax.axis_size(AXIS)
    levels = count.bit_length() - 1
    me = lax.axis_index(AXIS)
    high, top = 1 << levels - 2, 1 << levels - 1

    def swap(value, bit):
        return lax.ppermute(value, AXIS, [(i, i ^ 1 << bit) for i in range(count)])

    def send(value, real):
        return lax.ppermute(value, AXIS, fill(real, count))

    received = {bit: swap(keyval, bit) for bit in range(1, levels)}
    seeds = {holder: send(keyval, way(holder, side)) for holder, side in ((top, 4), (high | top, 2))}
    seeds = {top: seeds[top], high: received[levels - 2], high | top: seeds[high | top]}
    first = pick(seeds)
    own = hold(keyval, first)
    later = {4: received[2]}
    waves = plan(list(seeds), list(later), count)
    for k, wave in enumerate(waves):
        filled = first
        if k == 0:
            for holder, got in (later | {0: own}).items():
                filled = jnp.where(me == holder, got, filled)
        came = [(send(filled, wave[-1]), [t for _, t in wave[-1]])]
        came += [(send(first, real), [t for _, t in real]) for real in wave[:-1]]
        first = filled
        if k == 0:
            for bit in range(1, levels - 2):
                if 1 << bit not in later:
                    first = jnp.where(me == 1 << bit, received[bit], first)
            received[0] = jnp.where(member(me, [top, top ^ 4, 5]), seeds[high | top], seeds[top])
            received[0] = jnp.where(me == 1, came[0][0], received[0])
        if k + 1 == len(waves):
            *state, stacked = attend(queries, [own, *(received[bit] for bit in range(levels - 2, 1, -1))])
            *state, first = attend(stacked, [received[1]], state, carry=first)
            first = hold(first, received[levels - 1])
        for got, holders in came:
            first = jnp.where(member(me, holders), got, first)
    passed = swap(first, 0)
    state = attend(stacked, [received[levels - 1], received[0]], state)
    first = jnp.where(me % 2 == 1, passed, first)
    return attend(stacked, [first], state, last=True)[0]


def solution(mesh):
    return jax.shard_map(
        on_device,
        mesh=mesh,
        in_specs=(P(AXIS, None), P(None, AXIS, None)),
        out_specs=P(AXIS, None),
        check_vma=False,
    )
```
